128 devices in a mesh: traj: 16 (over y, x), tensor: 8 (over z, core).
Axes of the slice: x: 4, y: 4, z: 4, core: 2. Of those that a mesh axis runs over, the one named last changes fastest.
Arguments:
- ssm_in: bfloat16 [16, 256, 8192], P('traj', None, 'tensor'), may hold values from -6 to 6
- gate_in: bfloat16 [16, 256, 8192], P('traj', None, 'tensor'), may hold values from -6 to 6
- b_in: bfloat16 [16, 256, 2048], P('traj', None, 'tensor'), may hold values from -1.5 to 1.5
- c_in: bfloat16 [16, 256, 2048], P('traj', None, 'tensor'), may hold values from -1.5 to 1.5
- dt_in: float32 [16, 256, 128], P('traj', None, 'tensor'), may hold values from -5 to 5
- dt_bias: float32 [128], P('tensor'), may hold values from -2 to 0
- decay_rate: float32 [128], P('tensor'), may hold values from 0.005 to 0.25
- skip: float32 [128], P('tensor'), may hold values from 0.5 to 1.5
- norm_gain: float32 [8192], P('tensor'), may hold values from 0.5 to 1.5
- out_weight: bfloat16 [8192, 8192], P('tensor'), may hold values from -0.09375 to 0.09375
- state_roll: float32 [16, 128, 64, 256], P(None, 'tensor', 'traj'), may hold values from -4 to 4
- query: bfloat16 [16, 256, 8192], P('traj', None, 'tensor'), may hold values from -6 to 6
- new_kv: bfloat16 [2, 16, 256, 1024], P(None, 'traj', None, 'tensor'), may hold values from -6 to 6
- prefix_kv: bfloat16 [2, 16, 8192, 1024], P(None, None, ('traj', 'tensor')), may hold values from -6 to 6
- prefix_len: int32 [16], replicated, may hold values from 1024 to 8192, as said below
- order: int32 [16], replicated, may hold values from 0 to 15, each once
Outputs:
- mixed: bfloat16 [16, 256, 8192], P('traj', None, 'tensor')
- final_state: float32 [16, 128, 64, 256], P('traj', 'tensor')
- attended: bfloat16 [16, 256, 8192], P('traj', None, 'tensor')
The draws below stay inside these ranges and needn't reach their ends.
Inputs may be any that keep to these rules, and one draw needn't show every extreme that they name: `prefix_len`: some trajectory has exactly 8192 prefix positions. `order`: each rollout trajectory is taken by exactly one slot.
All inputs are finite; a program needn't handle non-finite values.
Results may differ from the reference program's by a relative error of at most 0.02.
Values may be sent and summed in bfloat16 or wider, within the bound.
No kernel may reach another device: no remote copies, remote signals or barrier semaphores. Data moves between devices by JAX's collectives and lax.ppermute only.
A program may use at most 128 MiB of HBM per device.

```python
import math
import jax
import jax.numpy as jnp
from jax import lax

D = 8192
HEADS = 128
HEAD_DIM = 64
STATE = 256
GROUPS = 8
QHEADS = 64
KVHEADS = 8
ATT_DIM = 128
SEG = 256
INNER = 8192
TRAJS = 16
PREFIX = 8192
N_TENSOR = 8


def shared_signs(key):
    sign_bits = jax.random.randint(jax.random.fold_in(key, 901), (KVHEADS, ATT_DIM), 0, 2)
    return (2 * sign_bits - 1).astype(jnp.float32)


def draw_prefix_len(key, part):
    key = jax.random.fold_in(key, 11)
    first_key, second_key = jax.random.split(key)
    lengths_drawn = jax.random.randint(first_key, (TRAJS,), PREFIX // 8, PREFIX + 1)
    where_full = jax.random.randint(second_key, (), 0, TRAJS)
    return lengths_drawn.at[where_full].set(PREFIX).astype(jnp.int32)


def draw_query(key, part):
    sign_pattern = shared_signs(key)
    key = jax.random.fold_in(key, 21)
    base_key, row_key = jax.random.split(key)
    full_shape = (TRAJS, SEG, QHEADS, ATT_DIM)
    drawn = jnp.clip(jax.random.normal(base_key, full_shape, jnp.float32), -6.0, 6.0)
    head_signs = jnp.repeat(sign_pattern, QHEADS // KVHEADS, axis=0)
    start_row = jax.random.randint(row_key, (TRAJS, 1, QHEADS), 0, SEG)
    positions = lax.broadcasted_iota(jnp.int32, (1, SEG, 1), 1)
    strength = jnp.zeros((TRAJS, SEG, QHEADS), jnp.float32)
    for level in range(4):
        target = (start_row + level * (SEG // 4)) % SEG
        strength = strength + jnp.where(positions == target, 3.0 + level, 0.0)
    planted = strength[..., None] * head_signs[None, None]
    result = jnp.where(strength[..., None] > 0.0, planted, drawn)
    return result.reshape(TRAJS, SEG, QHEADS * ATT_DIM).astype(jnp.bfloat16)


def draw_prefix_kv(key, part):
    sign_pattern = shared_signs(key)
    key = jax.random.fold_in(key, 31)
    base_key, first_key, gap_key = jax.random.split(key, 3)
    full_shape = (2, TRAJS, PREFIX, KVHEADS, ATT_DIM)
    drawn = jnp.clip(jax.random.normal(base_key, full_shape, jnp.float32), -6.0, 6.0)
    live_span = PREFIX // 8
    first_pos = jax.random.randint(first_key, (TRAJS, 1, KVHEADS), 0, live_span)
    second_pos = (first_pos + jax.random.randint(gap_key, (TRAJS, 1, KVHEADS), 1, live_span)) % live_span
    positions = lax.broadcasted_iota(jnp.int32, (1, PREFIX, 1), 1)
    lowered = max(1, ATT_DIM // 32)
    channel = lax.broadcasted_iota(jnp.int32, (KVHEADS, ATT_DIM), 1)
    key_high = 5.0 * sign_pattern
    key_near = jnp.where(channel < lowered, 4.0, 5.0) * sign_pattern
    planted_keys = jnp.where((positions == first_pos)[..., None], key_high[None, None], drawn[0])
    planted_keys = jnp.where((positions == second_pos)[..., None], key_near[None, None], planted_keys)
    result = jnp.stack([planted_keys, drawn[1]], axis=0)
    return result.reshape(2, TRAJS, PREFIX, KVHEADS * ATT_DIM).astype(jnp.bfloat16)


def spiked(array, rng, source, target, parts, factor):
    def block_of(position):
        return (jnp.arange(array.shape[position]) // (array.shape[position] // parts)).reshape((-1,) + (1,) * (array.ndim - 1 - position))

    near = jax.random.permutation(rng, parts)[block_of(target)]
    other_side = (block_of(target) + parts // 2) % parts
    return jnp.where((block_of(source) == near) | (block_of(source) == other_side), factor * array, array)


def shard_levels(stream_key, shape, cuts, low, largest):
    factor_of, own = 1.0, jax.random.fold_in(stream_key, 6)
    for axis_at, blocks in cuts:
        steps = jnp.exp(jax.random.uniform(jax.random.fold_in(own, axis_at), (blocks,), jnp.float32, low / len(cuts), largest / len(cuts)))
        factor_of = factor_of * jnp.repeat(steps, shape[axis_at] // blocks).reshape([-1 if axis == axis_at else 1 for axis in range(len(shape))])
    return factor_of


def bell_draw(rng, shape, deviation, most, shards=(), held_as=jnp.bfloat16):
    factor_of = shard_levels(rng, shape, shards, -0.22, 0.18) if shards else 1.0
    array = jax.random.normal(rng, shape, jnp.float32) * deviation * factor_of
    return jnp.minimum(jnp.maximum(array, -most), most).astype(held_as)


def gaussian_with(stream_key, shape, spread, reach, shards, heavy, kind=jnp.bfloat16):
    entries = spread * jax.random.normal(stream_key, shape, jnp.float32)
    if shards:
        entries = entries * shard_levels(stream_key, shape, shards, -0.22, 0.18)
    return jnp.clip(spiked(entries, jax.random.fold_in(stream_key, 3), *heavy), -reach, reach).astype(kind)


def setup_inputs(seed: int = 0) -> dict:
    seeds = jax.random.split(jax.random.key(seed), 17)
    return {
        "ssm_in": bell_draw(seeds[0], (TRAJS, SEG, INNER), 1.0, 6.0, ((0, 16), (2, 8))),
        "gate_in": bell_draw(seeds[1], (TRAJS, SEG, INNER), 1.0, 6.0, ((0, 16), (2, 8))),
        "b_in": bell_draw(seeds[2], (TRAJS, SEG, GROUPS * STATE), 0.25, 1.5, ((0, 16), (2, 8))),
        "c_in": bell_draw(seeds[3], (TRAJS, SEG, GROUPS * STATE), 0.25, 1.5, ((0, 16), (2, 8))),
        "dt_in": bell_draw(seeds[4], (TRAJS, SEG, HEADS), 1.0, 5.0, ((0, 16), (2, 8)), jnp.float32),
        "dt_bias": jnp.clip(-2.0 + 2.0 * jax.random.uniform(seeds[5], (HEADS,), jnp.float32) ** shard_levels(seeds[5], (HEADS,), ((0, 8),), -0.2, 0.2), -2.0, 0.0),
        "decay_rate": jnp.clip(jnp.exp(math.log(0.25) - 3.912023 * jax.random.uniform(seeds[6], (HEADS,), jnp.float32) ** shard_levels(seeds[6], (HEADS,), ((0, 8),), -0.2, 0.2)), 0.005, 0.25),
        "skip": jnp.clip(0.5 + 1.0 * jax.random.uniform(seeds[7], (HEADS,), jnp.float32) ** shard_levels(seeds[7], (HEADS,), ((0, 8),), -0.2, 0.2), 0.5, 1.5),
        "norm_gain": jnp.clip(1.0 + 0.1 * jax.random.normal(seeds[8], (INNER,), jnp.float32), 0.5, 1.5),
        "out_weight": gaussian_with(seeds[9], (INNER, D), INNER ** -0.5, 0.09375, ((0, 8),), (0, 1, 8, 2.0)),
        "state_roll": bell_draw(seeds[10], (TRAJS, HEADS, HEAD_DIM, STATE), 0.5, 4.0, ((1, 8), (2, 16)), jnp.float32),
        "query": draw_query(jax.random.fold_in(seeds[16], 71), 0),
        "new_kv": bell_draw(seeds[12], (2, TRAJS, SEG, KVHEADS * ATT_DIM), 1.0, 6.0, ((1, 16), (3, 8))),
        "prefix_kv": draw_prefix_kv(jax.random.fold_in(seeds[16], 71), 0),
        "prefix_len": draw_prefix_len(jax.random.fold_in(seeds[16], 71), 0),
        "order": jax.random.permutation(seeds[15], TRAJS).astype(jnp.int32),
    }


def mixer_core(ssm_x, gate_z, b_rows, c_rows, dt_raw, start_state, dt_bias, decay_rate, skip, norm_gain):
    seg = ssm_x.shape[0]
    heads = dt_raw.shape[1]
    groups = b_rows.shape[1] // STATE
    per_group = heads // groups
    step = jax.nn.softplus(dt_raw + dt_bias[None, :])
    cum = jnp.cumsum(-step * decay_rate[None, :], axis=0)
    rows_idx = lax.broadcasted_iota(jnp.int32, (seg, seg), 0)
    cols_idx = lax.broadcasted_iota(jnp.int32, (seg, seg), 1)
    causal = rows_idx >= cols_idx
    diff = cum[:, None, :] - cum[None, :, :]
    decay_mat = jnp.exp(jnp.where(causal[:, :, None], diff, -jnp.inf))
    x_heads = ssm_x.astype(jnp.float32).reshape(seg, heads, HEAD_DIM)
    b_plain = b_rows.reshape(seg, groups, STATE)
    c_plain = c_rows.reshape(seg, groups, STATE)
    b_group = b_plain.astype(jnp.float32)
    c_group = c_plain.astype(jnp.float32)
    b_heads = jnp.repeat(b_group, per_group, axis=1)
    c_heads = jnp.repeat(c_group, per_group, axis=1)
    inner = jnp.einsum('tgn,jgn->gtj', c_plain, b_plain, preferred_element_type=jnp.float32)
    inner_heads = jnp.repeat(inner, per_group, axis=0)
    mixing = jnp.transpose(decay_mat, (2, 0, 1)) * inner_heads * jnp.transpose(step)[:, None, :]
    out_y = jnp.einsum('htj,jhp->thp', mixing, x_heads, precision=lax.Precision.HIGHEST)
    carried = jnp.einsum('thn,hpn->thp', c_heads, start_state, precision=lax.Precision.HIGHEST)
    out_y = out_y + jnp.exp(cum)[:, :, None] * carried
    out_y = out_y + skip[None, :, None] * x_heads
    tail = jnp.exp(cum[-1][None, :] - cum) * step
    final = jnp.exp(cum[-1])[:, None, None] * start_state + jnp.einsum('jh,jhp,jhn->hpn', tail, x_heads, b_heads, precision=lax.Precision.HIGHEST)
    gated = out_y.reshape(seg, -1) * jax.nn.silu(gate_z.astype(jnp.float32))
    grouped = gated.reshape(seg, groups, -1)
    factor = lax.rsqrt(lax.optimization_barrier(jnp.mean(grouped * grouped, axis=-1, keepdims=True)) + 1e-05)
    normed = ((grouped * factor).reshape(seg, -1) * norm_gain[None, :]).astype(jnp.bfloat16)
    return (normed, final)

def attend(queries, keys, values, length, npre):
    seg = queries.shape[0]
    nkeys = keys.shape[0]
    qheads = queries.shape[1] // ATT_DIM
    kvheads = keys.shape[1] // ATT_DIM
    ratio = qheads // kvheads
    q_heads = jnp.transpose(queries.reshape(seg, qheads, ATT_DIM), (1, 0, 2))
    key_heads = keys.reshape(nkeys, kvheads, ATT_DIM)
    value_heads = values.reshape(nkeys, kvheads, ATT_DIM)
    kpos = lax.broadcasted_iota(jnp.int32, (seg, nkeys), 1)
    tpos = lax.broadcasted_iota(jnp.int32, (seg, nkeys), 0)
    valid = jnp.where(kpos < npre, kpos < length, kpos - npre <= tpos)
    factor = 1.0 / math.sqrt(ATT_DIM)

    def one_head(item):
        q_one, head = item
        kv_head = head // ratio
        k_one = lax.dynamic_index_in_dim(key_heads, kv_head, 1, keepdims=False)
        v_one = lax.dynamic_index_in_dim(value_heads, kv_head, 1, keepdims=False)
        score = lax.dot_general(q_one, k_one, (((1,), (1,)), ((), ())), preferred_element_type=jnp.float32) * factor
        score = jnp.where(valid, score, -jnp.inf)
        top = lax.optimization_barrier(jnp.max(score, axis=1, keepdims=True))
        expo = jnp.exp(score - top)
        total = lax.optimization_barrier(jnp.sum(expo, axis=1, keepdims=True))
        summed = jnp.dot(expo.astype(jnp.bfloat16), v_one, preferred_element_type=jnp.float32)
        return (summed / total).astype(jnp.bfloat16)
    result = lax.map(one_head, (q_heads, jnp.arange(qheads, dtype=jnp.int32)))
    return jnp.transpose(result, (1, 0, 2)).reshape(seg, -1)

def reference(ssm_in, gate_in, b_in, c_in, dt_in, dt_bias, decay_rate, skip, norm_gain, out_weight, state_roll, query, new_kv, prefix_kv, prefix_len, order):
    start_states = state_roll[order]
    lengths = prefix_len[order]
    pre_kv = prefix_kv[:, order]
    block = INNER // N_TENSOR

    def per_slot(item):
        ssm_x, gate_z, b_rows, c_rows, dt_raw, start_state = item
        normed, final = mixer_core(ssm_x, gate_z, b_rows, c_rows, dt_raw, start_state, dt_bias, decay_rate, skip, norm_gain)
        total = jnp.zeros((ssm_x.shape[0], D), jnp.float32)
        for part_idx in range(N_TENSOR):
            piece = jnp.dot(normed[:, part_idx * block:(part_idx + 1) * block], out_weight[part_idx * block:(part_idx + 1) * block], preferred_element_type=jnp.float32)
            rounded = lax.optimization_barrier(piece.astype(jnp.bfloat16))
            total = total + rounded.astype(jnp.float32)
        return (total.astype(jnp.bfloat16), final)
    mixed, final_state = lax.map(per_slot, (ssm_in, gate_in, b_in, c_in, dt_in, start_states))

    def per_slot_attention(item):
        queries, pre_keys, pre_values, new_keys, new_values, length = item
        keys = jnp.concatenate([pre_keys, new_keys], axis=0)
        values = jnp.concatenate([pre_values, new_values], axis=0)
        return attend(queries, keys, values, length, PREFIX)
    attended = lax.map(per_slot_attention, (query, pre_kv[0], pre_kv[1], new_kv[0], new_kv[1], lengths))
    return (mixed, final_state, attended)
```

```python
import functools
import math

import jax
import jax.numpy as jnp
from jax import lax
from jax.experimental import pallas as pl
from jax.experimental.pallas import tpu as pltpu
from jax.sharding import PartitionSpec as P

HEAD_DIM = 64
STATE = 256
ATT_DIM = 128
ROWS = 64
CHUNKS = ((0, 32), (32, 32))
KEY_BLOCK = 1024
VMEM_LIMIT = 48 * 1024 * 1024
NEG = -1e30


def pack_kernel(order_ref, kv_ref, *refs):
    outs, sem = refs[:-1], refs[-1]
    slots = kv_ref.shape[1]
    tensor = kv_ref.shape[3] // ATT_DIM

    def copies(slot):
        taken = order_ref[slot]
        for number, ((first, rows), out) in enumerate(zip(CHUNKS, outs)):
            for h in range(tensor):
                yield pltpu.make_async_copy(
                    kv_ref.at[:, taken, pl.ds(first, rows), pl.ds(h * ATT_DIM, ATT_DIM)],
                    out.at[slot * tensor + h],
                    sem.at[number],
                )

    for slot in range(slots):
        for copy in copies(slot):
            copy.start()
    for number, out in enumerate(outs):
        pltpu.make_async_copy(out, out, sem.at[number]).wait()


def pack(order, prefix_kv):
    slots = prefix_kv.shape[1]
    tensor = prefix_kv.shape[3] // ATT_DIM
    return pl.pallas_call(
        pack_kernel,
        out_shape=[
            jax.ShapeDtypeStruct((slots * tensor, 2, rows, ATT_DIM), jnp.bfloat16)
            for _, rows in CHUNKS
        ],
        in_specs=[pl.BlockSpec(memory_space=pltpu.SMEM), pl.BlockSpec(memory_space=pl.ANY)],
        out_specs=[pl.BlockSpec(memory_space=pl.ANY) for _ in CHUNKS],
        scratch_shapes=[pltpu.SemaphoreType.DMA((len(CHUNKS),))],
        compiler_params=pltpu.CompilerParams(vmem_limit_bytes=VMEM_LIMIT),
        cost_estimate=pl.CostEstimate(flops=0, bytes_accessed=8 << 20, transcendentals=0),
        name="pack_prefix",
    )(order, prefix_kv)


def mixer_kernel(
    x_ref, gate_ref, b_ref, c_ref, dt_ref, bias_ref, rate_ref, skip_ref, gain_ref, state_ref, w_ref,
    out_ref, final_ref, normed, y_ref, xt_ref,
):
    seg, width = x_ref.shape
    heads = dt_ref.shape[1]
    f32, bf16 = jnp.float32, jnp.bfloat16

    @pl.when(pl.program_id(0) == 0)
    def _():
        raw = dt_ref[...] + bias_ref[...]
        step = jnp.maximum(raw, 0.0) + jnp.log1p(jnp.exp(-jnp.abs(raw)))
        rows = lax.broadcasted_iota(jnp.int32, (seg, seg), 0)
        cols = lax.broadcasted_iota(jnp.int32, (seg, seg), 1)
        causal = rows >= cols
        lower = jnp.where(causal, 1.0, 0.0).astype(f32)
        pad = jnp.zeros((seg, 128 - heads), f32)
        decay = jnp.concatenate([-step * rate_ref[...], pad], axis=1)
        cum = jnp.dot(lower, decay, precision=lax.Precision.HIGHEST, preferred_element_type=f32)
        step = jnp.concatenate([step, pad], axis=1)
        cum_t = cum.T
        step_t = step.T
        last = cum[seg - 1 : seg, :]
        grow = jnp.exp(cum)
        tail = jnp.exp(last - cum) * step
        keep = jnp.exp(last)
        c = c_ref[...]
        b = b_ref[...]
        inner = lax.dot_general(c, b, (((1,), (1,)), ((), ())), preferred_element_type=f32)
        inner = jnp.where(causal, inner, 0.0)
        lane = lax.broadcasted_iota(jnp.int32, (seg, 128), 1)
        square = jnp.zeros((seg, 1), f32)
        for p in range(heads // 2):
            h = 2 * p
            span = pl.ds(p * 128, 128)
            x = x_ref[:, span]
            x_f = x.astype(f32)
            first = lane < HEAD_DIM

            def mixed_with(k):
                diff = jnp.minimum(cum[:, k : k + 1] - cum_t[k : k + 1, :], 0.0)
                mix = jnp.exp(diff) * inner * step_t[k : k + 1, :]
                return jnp.dot(mix.astype(bf16), x, preferred_element_type=f32)

            def spread(a):
                return jnp.where(first, a[:, h : h + 1], a[:, h + 1 : h + 2])

            carried = lax.dot_general(
                c, state_ref[span, :], (((1,), (1,)), ((), ())), preferred_element_type=f32
            )
            y = jnp.where(first, mixed_with(h), mixed_with(h + 1))
            y = y + spread(grow) * carried + skip_ref[:, span] * x_f
            gate = gate_ref[:, span].astype(f32)
            gated = y * (gate / (1.0 + jnp.exp(-gate)))
            y_ref[:, span] = gated
            square = square + jnp.sum(gated * gated, axis=1, keepdims=True)
            xt_ref[:, span] = (x_f * spread(tail)).astype(bf16)
        factor = lax.rsqrt(square / width + 1e-05)
        normed[...] = (y_ref[...] * factor * gain_ref[...]).astype(bf16)
        added = lax.dot_general(xt_ref[...], b, (((0,), (0,)), ((), ())), preferred_element_type=f32)
        for h in range(heads):
            span = pl.ds(h * HEAD_DIM, HEAD_DIM)
            final_ref[span, :] = (
                keep[:, h : h + 1] * state_ref[span, :].astype(f32)
                + added[h * HEAD_DIM : (h + 1) * HEAD_DIM]
            )

    out_ref[...] = jnp.dot(normed[...], w_ref[...], preferred_element_type=f32).astype(bf16)


def mixer(x, gate, b, c, dt, bias, rate, skip, gain, state, weight):
    seg, width = x.shape
    heads = dt.shape[1]
    total = weight.shape[1]
    block = 1024

    def whole(a):
        return pl.BlockSpec(a.shape, lambda i: (0,) * a.ndim)

    small = (
        x, gate, b, c, dt, bias[None], rate[None], jnp.repeat(skip, HEAD_DIM)[None], gain[None], state
    )
    return pl.pallas_call(
        mixer_kernel,
        grid=(total // block,),
        in_specs=[whole(a) for a in small] + [pl.BlockSpec((width, block), lambda i: (0, i))],
        out_specs=[
            pl.BlockSpec((seg, block), lambda i: (0, i)),
            pl.BlockSpec((width, STATE), lambda i: (0, 0)),
        ],
        out_shape=[
            jax.ShapeDtypeStruct((seg, total), jnp.bfloat16),
            jax.ShapeDtypeStruct((width, STATE), jnp.float32),
        ],
        scratch_shapes=[
            pltpu.VMEM((seg, width), jnp.bfloat16),
            pltpu.VMEM((seg, width), jnp.float32),
            pltpu.VMEM((seg, width), jnp.bfloat16),
        ],
        compiler_params=pltpu.CompilerParams(vmem_limit_bytes=VMEM_LIMIT),
        cost_estimate=pl.CostEstimate(
            flops=2 * seg * width * total + 4 * seg * seg * width,
            bytes_accessed=2 * width * total + 6 * seg * total,
            transcendentals=heads * seg * seg,
        ),
        name="mamba_mixer",
    )(*small, weight)


def attend_kernel(
    first_row, rows, first, last, length_ref, q_ref, kv_ref, *refs
):
    f32, bf16 = jnp.float32, jnp.bfloat16
    if first:
        new_ref, refs = refs[0], refs[1:]
        outs, refs = refs[: 1 if last else 3], refs[1 if last else 3 :]
    else:
        carry, outs, refs = refs[:3], refs[3 : 4 if last else 6], refs[4 if last else 6 :]
    top_ref, sum_ref, acc_ref, qt_ref = refs
    heads = q_ref.shape[1] // ATT_DIM
    seg = q_ref.shape[0]
    step = pl.program_id(0)
    sources = kv_ref.shape[0]
    block = sources * rows

    def scores(h, keys2):
        return jnp.dot(keys2, qt_ref[h], preferred_element_type=f32)

    def update(keys, values, mask, start):
        keys2 = jnp.concatenate([keys, keys], axis=1)
        size = values.shape[0]
        ones = jnp.ones((size, 16), bf16)
        values_t = jnp.concatenate([values.T, ones.T], axis=0)
        for h in range(heads):
            s = scores(h, keys2)
            if mask is not None:
                s = jnp.where(mask, s, NEG)
            peak = jnp.max(s, axis=0, keepdims=True)
            if start:
                top = peak
            else:
                old = top_ref[h : h + 1, :]
                top = jnp.maximum(old, peak)
                scale = jnp.exp2(old - top)
            top_ref[h : h + 1, :] = top
            weights = jnp.exp2(s - top).astype(bf16)
            part = jnp.dot(values_t, weights, preferred_element_type=f32)
            if start:
                acc_ref[h] = part[:ATT_DIM]
                sum_ref[h : h + 1, :] = part[ATT_DIM : ATT_DIM + 1]
            else:
                acc_ref[h] = acc_ref[h] * scale + part[:ATT_DIM]
                sum_ref[h : h + 1, :] = (
                    sum_ref[h : h + 1, :] * scale + part[ATT_DIM : ATT_DIM + 1]
                )

    @pl.when(step == 0)
    def _():
        factor = math.log2(math.e) / math.sqrt(ATT_DIM)
        for h in range(heads):
            q = q_ref[:, h * ATT_DIM : (h + 1) * ATT_DIM].astype(f32).T * factor
            high = q.astype(bf16)
            qt_ref[h, :ATT_DIM, :] = high
            qt_ref[h, ATT_DIM:, :] = (q - high.astype(f32)).astype(bf16)
        if first:
            keys = lax.broadcasted_iota(jnp.int32, (seg, seg), 0)
            tokens = lax.broadcasted_iota(jnp.int32, (seg, seg), 1)
            update(new_ref[0], new_ref[1], keys <= tokens, True)
        else:
            top_ref[...] = carry[0][...]
            sum_ref[...] = carry[1][...]
            acc_ref[...] = carry[2][...]

    length = length_ref[0]
    start = step * sources * ROWS + first_row
    end = start + (sources - 1) * ROWS + rows

    def block_of(which):
        return kv_ref[:, which].reshape(block, ATT_DIM)

    @pl.when(end <= length)
    def _():
        update(block_of(0), block_of(1), None, False)

    @pl.when((start < length) & (end > length))
    def _():
        row = lax.broadcasted_iota(jnp.int32, (block, seg), 0)
        place = start + row // rows * ROWS + row % rows
        update(block_of(0), block_of(1), place < length, False)

    @pl.when(step == pl.num_programs(0) - 1)
    def _():
        if last:
            for h in range(heads):
                result = acc_ref[h] / sum_ref[h : h + 1, :]
                outs[0][:, h * ATT_DIM : (h + 1) * ATT_DIM] = result.T.astype(bf16)
        else:
            outs[0][...] = top_ref[...]
            outs[1][...] = sum_ref[...]
            outs[2][...] = acc_ref[...]


def attend(length, queries, kv, new_kv, carry, first_row, last):
    seg, width = queries.shape
    heads = width // ATT_DIM
    sources, _, rows, _ = kv.shape
    per = KEY_BLOCK // rows
    first = carry is None

    def whole(shape):
        return pl.BlockSpec(shape, lambda i, n: (0,) * len(shape))

    carried = ((heads, seg), (heads, seg), (heads, ATT_DIM, seg))
    more = (new_kv,) if first else carry
    outs = ((seg, width),) if last else carried
    kinds = (jnp.bfloat16,) if last else (jnp.float32,) * 3

    def at(i, n):
        return (jnp.minimum(i, (n[0] - 1 - first_row) // (per * ROWS)), 0, 0, 0)

    work = sources * rows * seg * heads
    result = pl.pallas_call(
        functools.partial(attend_kernel, first_row, rows, first, last),
        grid_spec=pltpu.PrefetchScalarGridSpec(
            num_scalar_prefetch=1,
            grid=(sources // per,),
            in_specs=[whole(queries.shape), pl.BlockSpec((per, 2, rows, ATT_DIM), at)]
            + [whole(a.shape) for a in more],
            out_specs=[whole(s) for s in outs],
            scratch_shapes=[
                pltpu.VMEM((heads, seg), jnp.float32),
                pltpu.VMEM((heads, seg), jnp.float32),
                pltpu.VMEM((heads, ATT_DIM, seg), jnp.float32),
                pltpu.VMEM((heads, 2 * ATT_DIM, seg), jnp.bfloat16),
            ],
        ),
        out_shape=[jax.ShapeDtypeStruct(s, k) for s, k in zip(outs, kinds)],
        compiler_params=pltpu.CompilerParams(vmem_limit_bytes=VMEM_LIMIT),
        cost_estimate=pl.CostEstimate(
            flops=8 * work * ATT_DIM, bytes_accessed=4 * sources * rows * ATT_DIM, transcendentals=work
        ),
        name="attend_chunk",
    )(length[None], queries, kv, *more)
    return result[0] if last else tuple(result)


def local(
    ssm_in,
    gate_in,
    b_in,
    c_in,
    dt_in,
    dt_bias,
    decay_rate,
    skip,
    norm_gain,
    out_weight,
    state_roll,
    query,
    new_kv,
    prefix_kv,
    prefix_len,
    order,
):
    slot = lax.axis_index("traj")
    taken = lax.dynamic_index_in_dim(order, slot, 0, keepdims=False)
    length = lax.dynamic_index_in_dim(prefix_len, taken, 0, keepdims=False)
    own_state = lax.all_to_all(
        state_roll[order].astype(jnp.bfloat16), "traj", split_axis=0, concat_axis=0, tiled=True
    )
    packed = pack(order, prefix_kv)
    received = [
        lax.all_to_all(part, ("traj", "tensor"), split_axis=0, concat_axis=0, tiled=True)
        for part in packed
    ]
    heads = dt_in.shape[2]
    state = jnp.transpose(own_state, (1, 0, 2, 3)).reshape(heads * HEAD_DIM, STATE)
    product, final = mixer(
        ssm_in[0],
        gate_in[0],
        b_in[0],
        c_in[0],
        dt_in[0],
        dt_bias,
        decay_rate,
        skip,
        norm_gain,
        state,
        out_weight,
    )
    mixed = lax.psum_scatter(product[None], "tensor", scatter_dimension=2, tiled=True)
    carry = None
    for number, (part, (first_row, _)) in enumerate(zip(received, CHUNKS)):
        last = number == len(CHUNKS) - 1
        carry = attend(length, query[0], part, new_kv[:, 0], carry, first_row, last)
    return (mixed, final.reshape(1, heads, HEAD_DIM, STATE), carry[None])


def solution(mesh):
    in_specs = (
        P("traj", None, "tensor"),
        P("traj", None, "tensor"),
        P("traj", None, "tensor"),
        P("traj", None, "tensor"),
        P("traj", None, "tensor"),
        P("tensor"),
        P("tensor"),
        P("tensor"),
        P("tensor"),
        P("tensor", None),
        P(None, "tensor", "traj", None),
        P("traj", None, "tensor"),
        P(None, "traj", None, "tensor"),
        P(None, None, ("traj", "tensor"), None),
        P(),
        P(),
    )
    out_specs = (
        P("traj", None, "tensor"),
        P("traj", "tensor", None, None),
        P("traj", None, "tensor"),
    )
    return jax.shard_map(local, mesh=mesh, in_specs=in_specs, out_specs=out_specs, check_vma=False)
```

```python
import functools
import math

import jax
import jax.numpy as jnp
from jax import lax
from jax.experimental import pallas as pl
from jax.experimental.pallas import tpu as pltpu
from jax.sharding import PartitionSpec as P

HEAD_DIM = 64
STATE = 256
ATT_DIM = 128
ROWS = 64
CHUNKS = ((0, 48), (48, 16))
KEY_SOURCES = 32
AHEAD = 2
VMEM_LIMIT = 48 * 1024 * 1024
NEG = -1e30


def pack_kernel(order_ref, kv_ref, *refs):
    outs, (held, in_sem, out_sem) = refs[:-3], refs[-3:]
    slots = kv_ref.shape[1]
    tensor = kv_ref.shape[3] // ATT_DIM

    def fetch(slot):
        return pltpu.make_async_copy(
            kv_ref.at[:, order_ref[slot]], held.at[slot], in_sem.at[slot]
        )

    for slot in range(slots):
        fetch(slot).start()
    for slot in range(slots):
        fetch(slot).wait()
        for number, ((first, rows), out) in enumerate(zip(CHUNKS, outs)):
            for h in range(tensor):
                pltpu.make_async_copy(
                    held.at[slot, :, pl.ds(first, rows), pl.ds(h * ATT_DIM, ATT_DIM)],
                    out.at[slot * tensor + h],
                    out_sem.at[number],
                ).start()
    for number, out in enumerate(outs):
        pltpu.make_async_copy(out, out, out_sem.at[number]).wait()


def pack(order, prefix_kv):
    slots = prefix_kv.shape[1]
    tensor = prefix_kv.shape[3] // ATT_DIM
    return pl.pallas_call(
        pack_kernel,
        out_shape=[
            jax.ShapeDtypeStruct((slots * tensor, 2, rows, ATT_DIM), jnp.bfloat16)
            for _, rows in CHUNKS
        ],
        in_specs=[pl.BlockSpec(memory_space=pltpu.SMEM), pl.BlockSpec(memory_space=pl.ANY)],
        out_specs=[pl.BlockSpec(memory_space=pl.ANY) for _ in CHUNKS],
        scratch_shapes=[
            pltpu.VMEM((slots, 2) + prefix_kv.shape[2:], jnp.bfloat16),
            pltpu.SemaphoreType.DMA((slots,)),
            pltpu.SemaphoreType.DMA((len(CHUNKS),)),
        ],
        compiler_params=pltpu.CompilerParams(vmem_limit_bytes=VMEM_LIMIT),
        cost_estimate=pl.CostEstimate(flops=0, bytes_accessed=8 << 20, transcendentals=0),
        name="pack_prefix",
    )(order, prefix_kv)


def mixer_kernel(
    x_ref, gate_ref, b_ref, c_ref, dt_ref, bias_ref, rate_ref, skip_ref, gain_ref, state_ref, w_ref,
    out_ref, final_ref, normed, y_ref, xt_ref,
):
    seg, width = x_ref.shape
    heads = dt_ref.shape[1]
    f32, bf16 = jnp.float32, jnp.bfloat16

    @pl.when(pl.program_id(0) == 0)
    def _():
        raw = dt_ref[...] + bias_ref[...]
        step = jnp.maximum(raw, 0.0) + jnp.log1p(jnp.exp(-jnp.abs(raw)))
        rows = lax.broadcasted_iota(jnp.int32, (seg, seg), 0)
        cols = lax.broadcasted_iota(jnp.int32, (seg, seg), 1)
        causal = rows >= cols
        lower = jnp.where(causal, 1.0, 0.0).astype(f32)
        pad = jnp.zeros((seg, 128 - heads), f32)
        decay = jnp.concatenate([-step * rate_ref[...], pad], axis=1)
        cum = jnp.dot(lower, decay, precision=lax.Precision.HIGHEST, preferred_element_type=f32)
        step = jnp.concatenate([step, pad], axis=1)
        cum_t = cum.T
        step_t = step.T
        last = cum[seg - 1 : seg, :]
        grow = jnp.exp(cum)
        tail = jnp.exp(last - cum) * step
        keep = jnp.exp(last)
        c = c_ref[...]
        b = b_ref[...]
        inner = lax.dot_general(c, b, (((1,), (1,)), ((), ())), preferred_element_type=f32)
        inner = jnp.where(causal, inner, 0.0)
        lane = lax.broadcasted_iota(jnp.int32, (seg, 128), 1)
        square = jnp.zeros((seg, 1), f32)
        for p in range(heads // 2):
            h = 2 * p
            span = pl.ds(p * 128, 128)
            x = x_ref[:, span]
            x_f = x.astype(f32)
            first = lane < HEAD_DIM

            def mixed_with(k):
                diff = jnp.minimum(cum[:, k : k + 1] - cum_t[k : k + 1, :], 0.0)
                mix = jnp.exp(diff) * inner * step_t[k : k + 1, :]
                return jnp.dot(mix.astype(bf16), x, preferred_element_type=f32)

            def spread(a):
                return jnp.where(first, a[:, h : h + 1], a[:, h + 1 : h + 2])

            carried = lax.dot_general(
                c, state_ref[span, :], (((1,), (1,)), ((), ())), preferred_element_type=f32
            )
            y = jnp.where(first, mixed_with(h), mixed_with(h + 1))
            y = y + spread(grow) * carried + skip_ref[:, span] * x_f
            gate = gate_ref[:, span].astype(f32)
            gated = y * (gate / (1.0 + jnp.exp(-gate)))
            y_ref[:, span] = gated
            square = square + jnp.sum(gated * gated, axis=1, keepdims=True)
            xt_ref[:, span] = (x_f * spread(tail)).astype(bf16)
        factor = lax.rsqrt(square / width + 1e-05)
        normed[...] = (y_ref[...] * factor * gain_ref[...]).astype(bf16)
        added = lax.dot_general(xt_ref[...], b, (((0,), (0,)), ((), ())), preferred_element_type=f32)
        for h in range(heads):
            span = pl.ds(h * HEAD_DIM, HEAD_DIM)
            final_ref[span, :] = (
                keep[:, h : h + 1] * state_ref[span, :].astype(f32)
                + added[h * HEAD_DIM : (h + 1) * HEAD_DIM]
            )

    out_ref[...] = jnp.dot(normed[...], w_ref[...], preferred_element_type=f32).astype(bf16)


def mixer(x, gate, b, c, dt, bias, rate, skip, gain, state, weight):
    seg, width = x.shape
    heads = dt.shape[1]
    total = weight.shape[1]
    block = 1024

    def whole(a):
        return pl.BlockSpec(a.shape, lambda i: (0,) * a.ndim)

    small = (
        x, gate, b, c, dt, bias[None], rate[None], jnp.repeat(skip, HEAD_DIM)[None], gain[None], state
    )
    return pl.pallas_call(
        mixer_kernel,
        grid=(total // block,),
        in_specs=[whole(a) for a in small] + [pl.BlockSpec((width, block), lambda i: (0, i))],
        out_specs=[
            pl.BlockSpec((seg, block), lambda i: (0, i)),
            pl.BlockSpec((width, STATE), lambda i: (0, 0)),
        ],
        out_shape=[
            jax.ShapeDtypeStruct((seg, total), jnp.bfloat16),
            jax.ShapeDtypeStruct((width, STATE), jnp.float32),
        ],
        scratch_shapes=[
            pltpu.VMEM((seg, width), jnp.bfloat16),
            pltpu.VMEM((seg, width), jnp.float32),
            pltpu.VMEM((seg, width), jnp.bfloat16),
        ],
        compiler_params=pltpu.CompilerParams(vmem_limit_bytes=VMEM_LIMIT),
        cost_estimate=pl.CostEstimate(
            flops=2 * seg * width * total + 4 * seg * seg * width,
            bytes_accessed=2 * width * total + 6 * seg * total,
            transcendentals=heads * seg * seg,
        ),
        name="mamba_mixer",
    )(*small, weight)


def attend_kernel(
    first_row, rows, first, last, length_ref, q_ref, kv_ref, *refs
):
    f32, bf16 = jnp.float32, jnp.bfloat16
    if first:
        new_ref, refs = refs[0], refs[1:]
        outs, refs = refs[: 1 if last else 3], refs[1 if last else 3 :]
    else:
        carry, outs, refs = refs[:3], refs[3 : 4 if last else 6], refs[4 if last else 6 :]
    top_ref, sum_ref, acc_ref, qt_ref = refs
    heads = q_ref.shape[1] // ATT_DIM
    seg = q_ref.shape[0]
    step = pl.program_id(0)
    sources = kv_ref.shape[0]
    block = sources * rows

    def update(keys, values, mask, start):
        keys2 = jnp.concatenate([keys, keys], axis=1)
        size = values.shape[0]
        ones = jnp.ones((size, 16), bf16)
        values_t = jnp.concatenate([values.T, ones.T], axis=0)

        def score(h):
            s = jnp.dot(keys2, qt_ref[h], preferred_element_type=f32)
            if mask is not None:
                s = jnp.where(mask, s, NEG)
            return s, jnp.max(s, axis=0, keepdims=True)

        ahead = [score(h) for h in range(AHEAD)]
        for h in range(heads):
            if h + AHEAD < heads:
                ahead.append(score(h + AHEAD))
            s, peak = ahead.pop(0)
            if start:
                top = peak
            else:
                old = top_ref[h : h + 1, :]
                top = jnp.maximum(old, peak)
                scale = jnp.exp2(old - top)
            top_ref[h : h + 1, :] = top
            weights = jnp.exp2(s - top).astype(bf16)
            part = jnp.dot(values_t, weights, preferred_element_type=f32)
            if start:
                acc_ref[h] = part[:ATT_DIM]
                sum_ref[h : h + 1, :] = part[ATT_DIM : ATT_DIM + 1]
            else:
                acc_ref[h] = acc_ref[h] * scale + part[:ATT_DIM]
                sum_ref[h : h + 1, :] = (
                    sum_ref[h : h + 1, :] * scale + part[ATT_DIM : ATT_DIM + 1]
                )

    @pl.when(step == 0)
    def _():
        factor = math.log2(math.e) / math.sqrt(ATT_DIM)
        for h in range(heads):
            q = q_ref[:, h * ATT_DIM : (h + 1) * ATT_DIM].astype(f32).T * factor
            high = q.astype(bf16)
            qt_ref[h, :ATT_DIM, :] = high
            qt_ref[h, ATT_DIM:, :] = (q - high.astype(f32)).astype(bf16)
        if first:
            keys = lax.broadcasted_iota(jnp.int32, (seg, seg), 0)
            tokens = lax.broadcasted_iota(jnp.int32, (seg, seg), 1)
            update(new_ref[0], new_ref[1], keys <= tokens, True)
        else:
            top_ref[...] = carry[0][...]
            sum_ref[...] = carry[1][...]
            acc_ref[...] = carry[2][...]

    length = length_ref[0]
    start = step * sources * ROWS + first_row
    end = start + (sources - 1) * ROWS + rows

    def block_of(which):
        return kv_ref[:, which].reshape(block, ATT_DIM)

    @pl.when(end <= length)
    def _():
        update(block_of(0), block_of(1), None, False)

    @pl.when((start < length) & (end > length))
    def _():
        row = lax.broadcasted_iota(jnp.int32, (block, seg), 0)
        place = start + row // rows * ROWS + row % rows
        update(block_of(0), block_of(1), place < length, False)

    @pl.when(step == pl.num_programs(0) - 1)
    def _():
        if last:
            for h in range(heads):
                result = acc_ref[h] / sum_ref[h : h + 1, :]
                outs[0][:, h * ATT_DIM : (h + 1) * ATT_DIM] = result.T.astype(bf16)
        else:
            outs[0][...] = top_ref[...]
            outs[1][...] = sum_ref[...]
            outs[2][...] = acc_ref[...]


def attend(length, queries, kv, new_kv, carry, first_row, last):
    seg, width = queries.shape
    heads = width // ATT_DIM
    sources, _, rows, _ = kv.shape
    per = KEY_SOURCES
    first = carry is None

    def whole(shape):
        return pl.BlockSpec(shape, lambda i, n: (0,) * len(shape))

    carried = ((heads, seg), (heads, seg), (heads, ATT_DIM, seg))
    more = (new_kv,) if first else carry
    outs = ((seg, width),) if last else carried
    kinds = (jnp.bfloat16,) if last else (jnp.float32,) * 3

    def at(i, n):
        return (jnp.minimum(i, (n[0] - 1 - first_row) // (per * ROWS)), 0, 0, 0)

    work = sources * rows * seg * heads
    result = pl.pallas_call(
        functools.partial(attend_kernel, first_row, rows, first, last),
        grid_spec=pltpu.PrefetchScalarGridSpec(
            num_scalar_prefetch=1,
            grid=(sources // per,),
            in_specs=[whole(queries.shape), pl.BlockSpec((per, 2, rows, ATT_DIM), at)]
            + [whole(a.shape) for a in more],
            out_specs=[whole(s) for s in outs],
            scratch_shapes=[
                pltpu.VMEM((heads, seg), jnp.float32),
                pltpu.VMEM((heads, seg), jnp.float32),
                pltpu.VMEM((heads, ATT_DIM, seg), jnp.float32),
                pltpu.VMEM((heads, 2 * ATT_DIM, seg), jnp.bfloat16),
            ],
        ),
        out_shape=[jax.ShapeDtypeStruct(s, k) for s, k in zip(outs, kinds)],
        compiler_params=pltpu.CompilerParams(vmem_limit_bytes=VMEM_LIMIT),
        cost_estimate=pl.CostEstimate(
            flops=64 * work * ATT_DIM, bytes_accessed=4 * sources * rows * ATT_DIM, transcendentals=work
        ),
        name="attend_chunk",
    )(length[None], queries, kv, *more)
    return result[0] if last else tuple(result)


def local(
    ssm_in,
    gate_in,
    b_in,
    c_in,
    dt_in,
    dt_bias,
    decay_rate,
    skip,
    norm_gain,
    out_weight,
    state_roll,
    query,
    new_kv,
    prefix_kv,
    prefix_len,
    order,
):
    slot = lax.axis_index("traj")
    taken = lax.dynamic_index_in_dim(order, slot, 0, keepdims=False)
    length = lax.dynamic_index_in_dim(prefix_len, taken, 0, keepdims=False)
    own_state = lax.all_to_all(
        state_roll[order].astype(jnp.bfloat16), "traj", split_axis=0, concat_axis=0, tiled=True
    )
    received, before = [], own_state
    for part in pack(order, prefix_kv):
        before, part = lax.optimization_barrier((before, part))
        if received:
            received[-1] = before
        else:
            own_state = before
        before = lax.all_to_all(part, ("traj", "tensor"), split_axis=0, concat_axis=0, tiled=True)
        received.append(before)
    heads = dt_in.shape[2]
    state = jnp.transpose(own_state, (1, 0, 2, 3)).reshape(heads * HEAD_DIM, STATE)
    product, final = mixer(
        ssm_in[0],
        gate_in[0],
        b_in[0],
        c_in[0],
        dt_in[0],
        dt_bias,
        decay_rate,
        skip,
        norm_gain,
        state,
        out_weight,
    )
    mixed = lax.psum_scatter(product[None], "tensor", scatter_dimension=2, tiled=True)
    carry = None
    for number, (part, (first_row, _)) in enumerate(zip(received, CHUNKS)):
        last = number == len(CHUNKS) - 1
        carry = attend(length, query[0], part, new_kv[:, 0], carry, first_row, last)
    return (mixed, final.reshape(1, heads, HEAD_DIM, STATE), carry[None])


def solution(mesh):
    in_specs = (
        P("traj", None, "tensor"),
        P("traj", None, "tensor"),
        P("traj", None, "tensor"),
        P("traj", None, "tensor"),
        P("traj", None, "tensor"),
        P("tensor"),
        P("tensor"),
        P("tensor"),
        P("tensor"),
        P("tensor", None),
        P(None, "tensor", "traj", None),
        P("traj", None, "tensor"),
        P(None, "traj", None, "tensor"),
        P(None, None, ("traj", "tensor"), None),
        P(),
        P(),
    )
    out_specs = (
        P("traj", None, "tensor"),
        P("traj", "tensor", None, None),
        P("traj", None, "tensor"),
    )
    return jax.shard_map(local, mesh=mesh, in_specs=in_specs, out_specs=out_specs, check_vma=False)
```

```python
import functools
import math

import jax
import jax.numpy as jnp
from jax import lax
from jax.experimental import pallas as pl
from jax.experimental.pallas import tpu as pltpu
from jax.sharding import PartitionSpec as P

HEAD_DIM = 64
STATE = 256
ATT_DIM = 128
ROWS = 64
CHUNKS = ((0, 48, 32), (48, 16, 128))
VMEM_LIMIT = 56 * 1024 * 1024
AHEAD = 3
NEG = -1e30


def pack_kernel(order_ref, kv_ref, *refs):
    outs, (held, in_sem, out_sem) = refs[:-3], refs[-3:]
    slots = kv_ref.shape[1]
    tensor = kv_ref.shape[3] // ATT_DIM

    def fetch(slot):
        return pltpu.make_async_copy(
            kv_ref.at[:, order_ref[slot]], held.at[slot], in_sem.at[slot]
        )

    for slot in range(slots):
        fetch(slot).start()
    for slot in range(slots):
        fetch(slot).wait()
        for number, ((first, rows, _), out) in enumerate(zip(CHUNKS, outs)):
            for h in range(tensor):
                pltpu.make_async_copy(
                    held.at[slot, :, pl.ds(first, rows), pl.ds(h * ATT_DIM, ATT_DIM)],
                    out.at[slot * tensor + h],
                    out_sem.at[number],
                ).start()
    for number, out in enumerate(outs):
        pltpu.make_async_copy(out, out, out_sem.at[number]).wait()


def pack(order, prefix_kv):
    slots = prefix_kv.shape[1]
    tensor = prefix_kv.shape[3] // ATT_DIM
    return pl.pallas_call(
        pack_kernel,
        out_shape=[
            pltpu.HBM((slots * tensor, 2, rows, ATT_DIM), jnp.bfloat16) for _, rows, _ in CHUNKS
        ],
        in_specs=[pl.BlockSpec(memory_space=pltpu.SMEM), pl.BlockSpec(memory_space=pltpu.HBM)],
        out_specs=[pl.BlockSpec(memory_space=pltpu.HBM) for _ in CHUNKS],
        scratch_shapes=[
            pltpu.VMEM((slots, 2) + prefix_kv.shape[2:], jnp.bfloat16),
            pltpu.SemaphoreType.DMA((slots,)),
            pltpu.SemaphoreType.DMA((len(CHUNKS),)),
        ],
        compiler_params=pltpu.CompilerParams(vmem_limit_bytes=VMEM_LIMIT),
        cost_estimate=pl.CostEstimate(flops=0, bytes_accessed=8 << 20, transcendentals=0),
        name="pack_prefix",
    )(order, prefix_kv)


def mixer_kernel(
    first_ref,
    x_ref, gate_ref, b_ref, c_ref, dt_ref, bias_ref, rate_ref, skip_ref, gain_ref, state_ref, w_ref,
    out_ref, normed, final_ref, y_ref, xt_ref, w_held, w_sem,
):
    seg, width = x_ref.shape
    heads = dt_ref.shape[1]
    block = out_ref.shape[2]
    blocks = w_held.shape[0]
    f32, bf16 = jnp.float32, jnp.bfloat16
    at = pl.program_id(0)

    def fetch(i):
        span = pl.ds(pl.multiple_of((2 * i + first_ref[0]) * block, block), block)
        return pltpu.make_async_copy(w_ref.at[:, span], w_held.at[i], w_sem.at[i])

    @pl.when(at == 0)
    def _():
        for i in range(blocks):
            fetch(i).start()
        raw = dt_ref[...] + bias_ref[...]
        step = jnp.maximum(raw, 0.0) + jnp.log1p(jnp.exp(-jnp.abs(raw)))
        rows = lax.broadcasted_iota(jnp.int32, (seg, seg), 0)
        cols = lax.broadcasted_iota(jnp.int32, (seg, seg), 1)
        causal = rows >= cols
        lower = jnp.where(causal, 1.0, 0.0).astype(f32)
        pad = jnp.zeros((seg, 128 - heads), f32)
        decay = jnp.concatenate([-step * (rate_ref[...] * math.log2(math.e)), pad], axis=1)
        cum = jnp.dot(lower, decay, precision=lax.Precision.HIGHEST, preferred_element_type=f32)
        behind = cum - jnp.log2(jnp.concatenate([step, pad + 1.0], axis=1))
        behind_t = behind.T
        last = cum[seg - 1 : seg, :]
        grow = jnp.exp2(cum)
        tail = jnp.exp2(last - behind)
        c = c_ref[...]
        b = b_ref[...]
        inner = lax.dot_general(c, b, (((1,), (1,)), ((), ())), preferred_element_type=f32)
        lane = lax.broadcasted_iota(jnp.int32, (seg, 128), 1)
        first = lane < HEAD_DIM
        square = jnp.zeros((seg, 128), f32)
        for p in range(heads // 2):
            h = 2 * p
            span = pl.ds(p * 128, 128)
            x = x_ref[:, span]
            x_f = x.astype(f32)

            def mixed_with(k):
                diff = jnp.where(causal, cum[:, k : k + 1] - behind_t[k : k + 1, :], NEG)
                mix = jnp.exp2(diff) * inner
                return jnp.dot(mix.astype(bf16), x, preferred_element_type=f32)

            def spread(a):
                return jnp.where(first, a[:, h : h + 1], a[:, h + 1 : h + 2])

            carried = lax.dot_general(
                c, state_ref[span, :], (((1,), (1,)), ((), ())), preferred_element_type=f32
            )
            y = jnp.where(first, mixed_with(h), mixed_with(h + 1))
            y = y + spread(grow) * carried + skip_ref[:, span] * x_f
            gate = gate_ref[:, span].astype(f32)
            gated = y * (gate / (1.0 + jnp.exp(-gate)))
            y_ref[:, span] = gated
            square = square + gated * gated
            xt_ref[:, span] = (x_f * spread(tail)).astype(bf16)
        total = jnp.sum(square, axis=1, keepdims=True)
        factor = lax.rsqrt(total / width + 1e-05)
        normed[...] = (y_ref[...] * factor * gain_ref[...]).astype(bf16)

    @pl.when(at == pl.num_programs(0) - 1)
    def _():
        b = b_ref[...]
        raw = dt_ref[...] + bias_ref[...]
        step = jnp.maximum(raw, 0.0) + jnp.log1p(jnp.exp(-jnp.abs(raw)))
        keep = jnp.exp(-jnp.sum(step * rate_ref[...], axis=0, keepdims=True))
        added = lax.dot_general(xt_ref[...], b, (((0,), (0,)), ((), ())), preferred_element_type=f32)
        for h in range(heads):
            span = pl.ds(h * HEAD_DIM, HEAD_DIM)
            final_ref[span, :] = (
                keep[:, h : h + 1] * state_ref[span, :].astype(f32)
                + added[h * HEAD_DIM : (h + 1) * HEAD_DIM]
            )

    fetch(at).wait()
    out_ref[0] = jnp.dot(normed[...], w_held[at], preferred_element_type=f32).astype(bf16)


def project_kernel(first_ref, normed_ref, w_ref, arrived_ref, out_ref, w_held, w_sem):
    half, _, block = w_held.shape
    at = pl.program_id(0)

    def fetch(i):
        span = pl.ds(pl.multiple_of((2 * i + first_ref[0]) * block, block), block)
        return pltpu.make_async_copy(w_ref.at[:, span], w_held.at[i], w_sem.at[i])

    @pl.when(at == 0)
    def _():
        for i in range(half):
            fetch(i).start()

    fetch(at).wait()
    product = jnp.dot(normed_ref[...], w_held[at], preferred_element_type=jnp.float32)
    out_ref[0] = (product + arrived_ref[0].astype(jnp.float32)).astype(jnp.bfloat16)


def project(first, normed, weight, arrived):
    seg, width = normed.shape
    half, _, block = arrived.shape
    return pl.pallas_call(
        project_kernel,
        grid_spec=pltpu.PrefetchScalarGridSpec(
            num_scalar_prefetch=1,
            grid=(half,),
            in_specs=[
                pl.BlockSpec((seg, width), lambda i, n: (0, 0)),
                pl.BlockSpec(memory_space=pltpu.HBM),
                pl.BlockSpec((1, seg, block), lambda i, n: (i, 0, 0)),
            ],
            out_specs=pl.BlockSpec((1, seg, block), lambda i, n: (i, 0, 0)),
            scratch_shapes=[
                pltpu.VMEM((half, width, block), jnp.bfloat16),
                pltpu.SemaphoreType.DMA((half,)),
            ],
        ),
        out_shape=pltpu.HBM((half, seg, block), jnp.bfloat16),
        compiler_params=pltpu.CompilerParams(vmem_limit_bytes=VMEM_LIMIT),
        cost_estimate=pl.CostEstimate(
            flops=2 * seg * width * half * block,
            bytes_accessed=2 * width * half * block + 4 * half * seg * block,
            transcendentals=0,
        ),
        name="project_half",
    )(first, normed, weight, arrived)


def mixer(first, x, gate, b, c, dt, bias, rate, skip, gain, state, weight):
    seg, width = x.shape
    heads = dt.shape[1]
    block = 1024
    half = weight.shape[1] // block // 2

    def whole(a):
        return pl.BlockSpec(a.shape, lambda i, n: (0,) * a.ndim)

    small = (
        x, gate, b, c, dt, bias[None], rate[None], jnp.repeat(skip, HEAD_DIM)[None], gain[None], state
    )
    return pl.pallas_call(
        mixer_kernel,
        grid_spec=pltpu.PrefetchScalarGridSpec(
            num_scalar_prefetch=1,
            grid=(half,),
            in_specs=[whole(a) for a in small] + [pl.BlockSpec(memory_space=pltpu.HBM)],
            out_specs=[
                pl.BlockSpec((1, seg, block), lambda i, n: (i, 0, 0)),
                pl.BlockSpec((seg, width), lambda i, n: (0, 0)),
                pl.BlockSpec((width, STATE), lambda i, n: (0, 0)),
            ],
            scratch_shapes=[
                pltpu.VMEM((seg, width), jnp.float32),
                pltpu.VMEM((seg, width), jnp.bfloat16),
                pltpu.VMEM((half, width, block), jnp.bfloat16),
                pltpu.SemaphoreType.DMA((half,)),
            ],
        ),
        out_shape=[
            pltpu.HBM((half, seg, block), jnp.bfloat16),
            pltpu.HBM((seg, width), jnp.bfloat16),
            pltpu.HBM((width, STATE), jnp.float32),
        ],
        compiler_params=pltpu.CompilerParams(vmem_limit_bytes=VMEM_LIMIT),
        cost_estimate=pl.CostEstimate(
            flops=2 * seg * width * half * block + 4 * seg * seg * width,
            bytes_accessed=2 * width * half * block + 6 * seg * half * block,
            transcendentals=heads * seg * seg,
        ),
        name="mamba_mixer",
    )(first, *small, weight)


def update(qt_ref, top_ref, sum_ref, acc_ref, keys, values, mask, start):
    f32, bf16 = jnp.float32, jnp.bfloat16
    heads = acc_ref.shape[0]
    keys2 = jnp.concatenate([keys, keys], axis=1)
    size = values.shape[0]
    ones = jnp.ones((size, 16), bf16)
    values_t = jnp.concatenate([values.T, ones.T], axis=0)

    def score(h):
        s = jnp.dot(keys2, qt_ref[h], preferred_element_type=f32)
        if mask is not None:
            s = jnp.where(mask, s, NEG)
        return s, jnp.max(s, axis=0, keepdims=True)

    ahead = [score(h) for h in range(AHEAD)]
    for h in range(heads):
        if h + AHEAD < heads:
            ahead.append(score(h + AHEAD))
        s, peak = ahead.pop(0)
        if start:
            top = peak
        else:
            old = top_ref[h : h + 1, :]
            top = jnp.maximum(old, peak)
            scale = jnp.exp2(old - top)
        top_ref[h : h + 1, :] = top
        weights = jnp.exp2(s - top).astype(bf16)
        part = jnp.dot(values_t, weights, preferred_element_type=f32)
        if start:
            acc_ref[h] = part[:ATT_DIM]
            sum_ref[h : h + 1, :] = part[ATT_DIM : ATT_DIM + 1]
        else:
            acc_ref[h] = acc_ref[h] * scale + part[:ATT_DIM]
            sum_ref[h : h + 1, :] = (
                sum_ref[h : h + 1, :] * scale + part[ATT_DIM : ATT_DIM + 1]
            )


def attend_new_kernel(q_ref, new_ref, top_ref, sum_ref, acc_ref, qt_ref):
    f32, bf16 = jnp.float32, jnp.bfloat16
    seg = q_ref.shape[0]
    factor = math.log2(math.e) / math.sqrt(ATT_DIM)
    for h in range(qt_ref.shape[0]):
        q = q_ref[:, h * ATT_DIM : (h + 1) * ATT_DIM].astype(f32).T * factor
        high = q.astype(bf16)
        qt_ref[h, :ATT_DIM, :] = high
        qt_ref[h, ATT_DIM:, :] = (q - high.astype(f32)).astype(bf16)
    keys = lax.broadcasted_iota(jnp.int32, (seg, seg), 0)
    tokens = lax.broadcasted_iota(jnp.int32, (seg, seg), 1)
    update(
        qt_ref, top_ref, sum_ref, acc_ref, new_ref[0], new_ref[1], keys <= tokens, True
    )


def attend_new(queries, new_kv):
    seg, width = queries.shape
    heads = width // ATT_DIM
    vmem = pl.BlockSpec(memory_space=pltpu.VMEM)
    return pl.pallas_call(
        attend_new_kernel,
        in_specs=[vmem, vmem],
        out_specs=[vmem] * 4,
        out_shape=[
            pltpu.HBM((heads, seg), jnp.float32),
            pltpu.HBM((heads, seg), jnp.float32),
            pltpu.HBM((heads, ATT_DIM, seg), jnp.float32),
            pltpu.HBM((heads, 2 * ATT_DIM, seg), jnp.bfloat16),
        ],
        compiler_params=pltpu.CompilerParams(vmem_limit_bytes=VMEM_LIMIT),
        cost_estimate=pl.CostEstimate(
            flops=8 * seg * seg * width, bytes_accessed=16 * seg * width, transcendentals=seg * seg * heads
        ),
        name="attend_new",
    )(queries, new_kv)


def attend_kernel(
    first_row, rows, last, order_ref, length_ref, slot_ref, qt_ref, kv_ref, top_in, sum_in, acc_in, *refs
):
    bf16 = jnp.bfloat16
    outs, state = refs[:-3], refs[-3:]
    top_ref, sum_ref, acc_ref = state
    heads, _, seg = qt_ref.shape
    step = pl.program_id(0)
    sources = kv_ref.shape[0]
    block = sources * rows

    @pl.when(step == 0)
    def _():
        top_ref[...] = top_in[...]
        sum_ref[...] = sum_in[...]
        acc_ref[...] = acc_in[...]

    length = length_ref[order_ref[slot_ref[0]]]
    start = step * sources * ROWS + first_row
    end = start + (sources - 1) * ROWS + rows

    def block_of(which):
        return kv_ref[:, which].reshape(block, ATT_DIM)

    @pl.when(end <= length)
    def _():
        update(qt_ref, *state, block_of(0), block_of(1), None, False)

    @pl.when((start < length) & (end > length))
    def _():
        row = lax.broadcasted_iota(jnp.int32, (block, seg), 0)
        place = start + row // rows * ROWS + row % rows
        update(qt_ref, *state, block_of(0), block_of(1), place < length, False)

    @pl.when(step == pl.num_programs(0) - 1)
    def _():
        if last:
            for h in range(heads):
                result = acc_ref[h] / sum_ref[h : h + 1, :]
                outs[0][:, h * ATT_DIM : (h + 1) * ATT_DIM] = result.T.astype(bf16)
        else:
            outs[0][...] = top_ref[...]
            outs[1][...] = sum_ref[...]
            outs[2][...] = acc_ref[...]


def attend(order, prefix_len, slot, qt, kv, carry, first_row, per, last):
    heads, _, seg = qt.shape
    sources, _, rows, _ = kv.shape

    def whole(shape):
        return pl.BlockSpec(shape, lambda i, *_: (0,) * len(shape))

    qt, *carry = [pltpu.with_memory_space_constraint(a, pltpu.HBM) for a in (qt, *carry)]
    carried = [a.shape for a in carry]
    outs = [(seg, heads * ATT_DIM)] if last else carried
    kind = jnp.bfloat16 if last else jnp.float32

    def at(i, order, lengths, slot):
        length = lengths[order[slot[0]]]
        return (jnp.minimum(i, (length - 1 - first_row) // (per * ROWS)), 0, 0, 0)

    work = sources * rows * seg * heads
    result = pl.pallas_call(
        functools.partial(attend_kernel, first_row, rows, last),
        grid_spec=pltpu.PrefetchScalarGridSpec(
            num_scalar_prefetch=3,
            grid=(sources // per,),
            in_specs=[whole(qt.shape), pl.BlockSpec((per, 2, rows, ATT_DIM), at)]
            + [whole(s) for s in carried],
            out_specs=[whole(s) for s in outs],
            scratch_shapes=[pltpu.VMEM(s, jnp.float32) for s in carried],
        ),
        out_shape=[pltpu.HBM(s, kind) for s in outs],
        compiler_params=pltpu.CompilerParams(vmem_limit_bytes=(32 if last else 56) * 1024 * 1024),
        cost_estimate=pl.CostEstimate(
            flops=64 * work * ATT_DIM, bytes_accessed=4 * sources * rows * ATT_DIM, transcendentals=work
        ),
        name="attend_chunk",
    )(order, prefix_len, slot, qt, kv, *carry)
    return result[0] if last else tuple(result)


def local(
    ssm_in,
    gate_in,
    b_in,
    c_in,
    dt_in,
    dt_bias,
    decay_rate,
    skip,
    norm_gain,
    out_weight,
    state_roll,
    query,
    new_kv,
    prefix_kv,
    prefix_len,
    order,
):
    slot = lax.axis_index("traj")
    own_state = lax.all_to_all(
        state_roll.at[order]
        .get(mode="promise_in_bounds", wrap_negative_indices=False)
        .astype(jnp.bfloat16),
        "traj", split_axis=0, concat_axis=0, tiled=True
    )
    prefix_kv = pltpu.with_memory_space_constraint(prefix_kv, pltpu.HBM)
    received, ahead = [], own_state
    for part in pack(order, prefix_kv):
        ahead, part = lax.optimization_barrier((ahead, part))
        if received:
            received[-1] = ahead
        else:
            own_state = ahead
        ahead = lax.all_to_all(part, ("traj", "tensor"), split_axis=0, concat_axis=0, tiled=True)
        received.append(ahead)
    heads = dt_in.shape[2]
    state = jnp.transpose(own_state, (1, 0, 2, 3)).reshape(heads * HEAD_DIM, STATE)
    place = lax.axis_index("tensor")
    core = place % 2
    tensor = lax.axis_size("tensor")
    other, normed, final_state = mixer(
        (1 - core)[None],
        ssm_in[0],
        gate_in[0],
        b_in[0],
        c_in[0],
        dt_in[0],
        dt_bias,
        decay_rate,
        skip,
        norm_gain,
        state,
        out_weight,
    )
    arrived = lax.ppermute(other, "tensor", [(i, i ^ 1) for i in range(tensor)])
    *carry, qt = attend_new(query[0], new_kv[:, 0])
    normed, carry[0] = lax.optimization_barrier((normed, carry[0]))
    mixed = lax.psum_scatter(
        project(core[None], normed, out_weight, arrived),
        "tensor",
        scatter_dimension=0,
        tiled=True,
        axis_index_groups=[list(range(c, tensor, 2)) for c in range(2)],
    )
    for number, (part, (first_row, _, per)) in enumerate(zip(received, CHUNKS)):
        last = number == len(CHUNKS) - 1
        carry = attend(order, prefix_len, slot[None], qt, part, carry, first_row, per, last)
    return (mixed, final_state.reshape(1, heads, HEAD_DIM, STATE), carry[None])


def solution(mesh):
    in_specs = (
        P("traj", None, "tensor"),
        P("traj", None, "tensor"),
        P("traj", None, "tensor"),
        P("traj", None, "tensor"),
        P("traj", None, "tensor"),
        P("tensor"),
        P("tensor"),
        P("tensor"),
        P("tensor"),
        P("tensor", None),
        P(None, "tensor", "traj", None),
        P("traj", None, "tensor"),
        P(None, "traj", None, "tensor"),
        P(None, None, ("traj", "tensor"), None),
        P(),
        P(),
    )
    out_specs = (
        P("traj", None, "tensor"),
        P("traj", "tensor", None, None),
        P("traj", None, "tensor"),
    )
    return jax.shard_map(local, mesh=mesh, in_specs=in_specs, out_specs=out_specs, check_vma=False)
```

```python
import functools
import math

import jax
import jax.numpy as jnp
from jax import lax
from jax.experimental import pallas as pl
from jax.experimental.pallas import tpu as pltpu
from jax.sharding import PartitionSpec as P

HEAD_DIM = 64
STATE = 256
ATT_DIM = 128
ROWS = 64
CHUNKS = ((0, 48, 32), (48, 16, 128))
VMEM_LIMIT = 56 * 1024 * 1024
AHEAD = 3
NEG = -1e30


def pack_kernel(order_ref, kv_ref, *refs):
    outs, (held, in_sem, out_sem) = refs[:-3], refs[-3:]
    slots = kv_ref.shape[1]
    tensor = kv_ref.shape[3] // ATT_DIM

    def fetch(slot):
        return pltpu.make_async_copy(
            kv_ref.at[:, order_ref[slot]], held.at[slot], in_sem.at[slot]
        )

    for slot in range(slots):
        fetch(slot).start()
    for slot in range(slots):
        fetch(slot).wait()
        for number, ((first, rows, _), out) in enumerate(zip(CHUNKS, outs)):
            for h in range(tensor):
                pltpu.make_async_copy(
                    held.at[slot, :, pl.ds(first, rows), pl.ds(h * ATT_DIM, ATT_DIM)],
                    out.at[slot * tensor + h],
                    out_sem.at[number],
                ).start()
    for number, out in enumerate(outs):
        pltpu.make_async_copy(out, out, out_sem.at[number]).wait()


def pack(order, prefix_kv):
    slots = prefix_kv.shape[1]
    tensor = prefix_kv.shape[3] // ATT_DIM
    return pl.pallas_call(
        pack_kernel,
        out_shape=[
            pltpu.HBM((slots * tensor, 2, rows, ATT_DIM), jnp.bfloat16) for _, rows, _ in CHUNKS
        ],
        in_specs=[pl.BlockSpec(memory_space=pltpu.SMEM), pl.BlockSpec(memory_space=pltpu.HBM)],
        out_specs=[pl.BlockSpec(memory_space=pltpu.HBM) for _ in CHUNKS],
        scratch_shapes=[
            pltpu.VMEM((slots, 2) + prefix_kv.shape[2:], jnp.bfloat16),
            pltpu.SemaphoreType.DMA((slots,)),
            pltpu.SemaphoreType.DMA((len(CHUNKS),)),
        ],
        compiler_params=pltpu.CompilerParams(vmem_limit_bytes=VMEM_LIMIT),
        cost_estimate=pl.CostEstimate(flops=0, bytes_accessed=8 << 20, transcendentals=0),
        name="pack_prefix",
    )(order, prefix_kv)


def mixer_kernel(
    first_ref,
    x_ref, gate_ref, b_ref, c_ref, dt_ref, bias_ref, rate_ref, skip_ref, gain_ref, state_ref, w_ref,
    out_ref, normed, final_ref, y_ref, xt_ref, w_held, w_sem,
):
    seg, width = x_ref.shape
    heads = dt_ref.shape[1]
    block = out_ref.shape[2]
    blocks = w_held.shape[0]
    f32, bf16 = jnp.float32, jnp.bfloat16
    at = pl.program_id(0)

    def fetch(i):
        span = pl.ds(pl.multiple_of((2 * i + first_ref[0]) * block, block), block)
        return pltpu.make_async_copy(w_ref.at[:, span], w_held.at[i], w_sem.at[i])

    @pl.when(at == 0)
    def _():
        for i in range(blocks):
            fetch(i).start()
        raw = dt_ref[...] + bias_ref[...]
        step = jnp.maximum(raw, 0.0) + jnp.log1p(jnp.exp(-jnp.abs(raw)))
        rows = lax.broadcasted_iota(jnp.int32, (seg, seg), 0)
        cols = lax.broadcasted_iota(jnp.int32, (seg, seg), 1)
        causal = rows >= cols
        lower = jnp.where(causal, 1.0, 0.0).astype(f32)
        pad = jnp.zeros((seg, 128 - heads), f32)
        decay = jnp.concatenate([-step * (rate_ref[...] * math.log2(math.e)), pad], axis=1)
        cum = jnp.dot(lower, decay, precision=lax.Precision.HIGHEST, preferred_element_type=f32)
        behind = cum - jnp.log2(jnp.concatenate([step, pad + 1.0], axis=1))
        behind_t = behind.T
        last = cum[seg - 1 : seg, :]
        grow = jnp.exp2(cum)
        tail = jnp.exp2(last - behind)
        c = c_ref[...]
        b = b_ref[...]
        inner = lax.dot_general(c, b, (((1,), (1,)), ((), ())), preferred_element_type=f32)
        lane = lax.broadcasted_iota(jnp.int32, (seg, 128), 1)
        first = lane < HEAD_DIM
        square = jnp.zeros((seg, 128), f32)
        for p in range(heads // 2):
            h = 2 * p
            span = pl.ds(p * 128, 128)
            x = x_ref[:, span]
            x_f = x.astype(f32)

            def mixed_with(k):
                diff = jnp.where(causal, cum[:, k : k + 1] - behind_t[k : k + 1, :], NEG)
                mix = jnp.exp2(diff) * inner
                return jnp.dot(mix.astype(bf16), x, preferred_element_type=f32)

            def spread(a):
                return jnp.where(first, a[:, h : h + 1], a[:, h + 1 : h + 2])

            carried = lax.dot_general(
                c, state_ref[span, :], (((1,), (1,)), ((), ())), preferred_element_type=f32
            )
            y = jnp.where(first, mixed_with(h), mixed_with(h + 1))
            y = y + spread(grow) * carried + skip_ref[:, span] * x_f
            gate = gate_ref[:, span].astype(f32)
            gated = y * (gate / (1.0 + jnp.exp(-gate)))
            y_ref[:, span] = gated
            square = square + gated * gated
            xt_ref[:, span] = (x_f * spread(tail)).astype(bf16)
        total = jnp.sum(square, axis=1, keepdims=True)
        factor = lax.rsqrt(total / width + 1e-05)
        normed[...] = (y_ref[...] * factor * gain_ref[...]).astype(bf16)

    @pl.when(at == pl.num_programs(0) - 1)
    def _():
        b = b_ref[...]
        raw = dt_ref[...] + bias_ref[...]
        step = jnp.maximum(raw, 0.0) + jnp.log1p(jnp.exp(-jnp.abs(raw)))
        keep = jnp.exp(-jnp.sum(step * rate_ref[...], axis=0, keepdims=True))
        added = lax.dot_general(xt_ref[...], b, (((0,), (0,)), ((), ())), preferred_element_type=f32)
        for h in range(heads):
            span = pl.ds(h * HEAD_DIM, HEAD_DIM)
            final_ref[span, :] = (
                keep[:, h : h + 1] * state_ref[span, :].astype(f32)
                + added[h * HEAD_DIM : (h + 1) * HEAD_DIM]
            )

    fetch(at).wait()
    out_ref[0] = jnp.dot(normed[...], w_held[at], preferred_element_type=f32).astype(bf16)


def project_kernel(first_ref, normed_ref, w_ref, arrived_ref, out_ref, w_held, w_sem):
    half, _, block = w_held.shape
    at = pl.program_id(0)

    def fetch(i):
        span = pl.ds(pl.multiple_of((2 * i + first_ref[0]) * block, block), block)
        return pltpu.make_async_copy(w_ref.at[:, span], w_held.at[i], w_sem.at[i])

    @pl.when(at == 0)
    def _():
        for i in range(half):
            fetch(i).start()

    fetch(at).wait()
    product = jnp.dot(normed_ref[...], w_held[at], preferred_element_type=jnp.float32)
    out_ref[0] = (product + arrived_ref[0].astype(jnp.float32)).astype(jnp.bfloat16)


def project(first, normed, weight, arrived):
    seg, width = normed.shape
    half, _, block = arrived.shape
    return pl.pallas_call(
        project_kernel,
        grid_spec=pltpu.PrefetchScalarGridSpec(
            num_scalar_prefetch=1,
            grid=(half,),
            in_specs=[
                pl.BlockSpec((seg, width), lambda i, n: (0, 0)),
                pl.BlockSpec(memory_space=pltpu.HBM),
                pl.BlockSpec((1, seg, block), lambda i, n: (i, 0, 0)),
            ],
            out_specs=pl.BlockSpec((1, seg, block), lambda i, n: (i, 0, 0)),
            scratch_shapes=[
                pltpu.VMEM((half, width, block), jnp.bfloat16),
                pltpu.SemaphoreType.DMA((half,)),
            ],
        ),
        out_shape=pltpu.HBM((half, seg, block), jnp.bfloat16),
        compiler_params=pltpu.CompilerParams(vmem_limit_bytes=VMEM_LIMIT),
        cost_estimate=pl.CostEstimate(
            flops=2 * seg * width * half * block,
            bytes_accessed=2 * width * half * block + 4 * half * seg * block,
            transcendentals=0,
        ),
        name="project_half",
    )(first, normed, weight, arrived)


def mixer(first, x, gate, b, c, dt, bias, rate, skip, gain, state, weight):
    seg, width = x.shape
    heads = dt.shape[1]
    block = 1024
    half = weight.shape[1] // block // 2

    def whole(a):
        return pl.BlockSpec(a.shape, lambda i, n: (0,) * a.ndim)

    small = (
        x, gate, b, c, dt, bias[None], rate[None], jnp.repeat(skip, HEAD_DIM)[None], gain[None], state
    )
    return pl.pallas_call(
        mixer_kernel,
        grid_spec=pltpu.PrefetchScalarGridSpec(
            num_scalar_prefetch=1,
            grid=(half,),
            in_specs=[whole(a) for a in small] + [pl.BlockSpec(memory_space=pltpu.HBM)],
            out_specs=[
                pl.BlockSpec((1, seg, block), lambda i, n: (i, 0, 0)),
                pl.BlockSpec((seg, width), lambda i, n: (0, 0)),
                pl.BlockSpec((width, STATE), lambda i, n: (0, 0)),
            ],
            scratch_shapes=[
                pltpu.VMEM((seg, width), jnp.float32),
                pltpu.VMEM((seg, width), jnp.bfloat16),
                pltpu.VMEM((half, width, block), jnp.bfloat16),
                pltpu.SemaphoreType.DMA((half,)),
            ],
        ),
        out_shape=[
            pltpu.HBM((half, seg, block), jnp.bfloat16),
            pltpu.HBM((seg, width), jnp.bfloat16),
            pltpu.HBM((width, STATE), jnp.float32),
        ],
        compiler_params=pltpu.CompilerParams(vmem_limit_bytes=VMEM_LIMIT),
        cost_estimate=pl.CostEstimate(
            flops=2 * seg * width * half * block + 4 * seg * seg * width,
            bytes_accessed=2 * width * half * block + 6 * seg * half * block,
            transcendentals=heads * seg * seg,
        ),
        name="mamba_mixer",
    )(first, *small, weight)


def update(qt_ref, top_ref, sum_ref, acc_ref, keys, values, mask, start, olds=None):
    f32, bf16 = jnp.float32, jnp.bfloat16
    heads = acc_ref.shape[0]
    old_top, old_sum, old_acc = olds or (top_ref, sum_ref, acc_ref)
    keys2 = jnp.concatenate([keys, keys], axis=1)
    size = values.shape[0]
    ones = jnp.ones((size, 16), bf16)
    values_t = jnp.concatenate([values.T, ones.T], axis=0)

    def score(h):
        s = jnp.dot(keys2, qt_ref[h], preferred_element_type=f32)
        if mask is not None:
            s = jnp.where(mask, s, NEG)
        return s, jnp.max(s, axis=0, keepdims=True)

    ahead = [score(h) for h in range(AHEAD)]
    for h in range(heads):
        if h + AHEAD < heads:
            ahead.append(score(h + AHEAD))
        s, peak = ahead.pop(0)
        if start:
            top = peak
        else:
            old = old_top[h : h + 1, :]
            top = jnp.maximum(old, peak)
            scale = jnp.exp2(old - top)
        top_ref[h : h + 1, :] = top
        weights = jnp.exp2(s - top).astype(bf16)
        part = jnp.dot(values_t, weights, preferred_element_type=f32)
        if start:
            acc_ref[h] = part[:ATT_DIM]
            sum_ref[h : h + 1, :] = part[ATT_DIM : ATT_DIM + 1]
        else:
            acc_ref[h] = old_acc[h] * scale + part[:ATT_DIM]
            sum_ref[h : h + 1, :] = (
                old_sum[h : h + 1, :] * scale + part[ATT_DIM : ATT_DIM + 1]
            )


def attend_new_kernel(q_ref, new_ref, top_ref, sum_ref, acc_ref, qt_ref):
    f32, bf16 = jnp.float32, jnp.bfloat16
    seg = q_ref.shape[0]
    factor = math.log2(math.e) / math.sqrt(ATT_DIM)
    for h in range(qt_ref.shape[0]):
        q = q_ref[:, h * ATT_DIM : (h + 1) * ATT_DIM].astype(f32).T * factor
        high = q.astype(bf16)
        qt_ref[h, :ATT_DIM, :] = high
        qt_ref[h, ATT_DIM:, :] = (q - high.astype(f32)).astype(bf16)
    keys = lax.broadcasted_iota(jnp.int32, (seg, seg), 0)
    tokens = lax.broadcasted_iota(jnp.int32, (seg, seg), 1)
    update(
        qt_ref, top_ref, sum_ref, acc_ref, new_ref[0], new_ref[1], keys <= tokens, True
    )


def attend_new(queries, new_kv):
    seg, width = queries.shape
    heads = width // ATT_DIM
    vmem = pl.BlockSpec(memory_space=pltpu.VMEM)
    return pl.pallas_call(
        attend_new_kernel,
        in_specs=[vmem, vmem],
        out_specs=[vmem] * 4,
        out_shape=[
            pltpu.HBM((heads, seg), jnp.float32),
            pltpu.HBM((heads, seg), jnp.float32),
            pltpu.HBM((heads, ATT_DIM, seg), jnp.float32),
            pltpu.HBM((heads, 2 * ATT_DIM, seg), jnp.bfloat16),
        ],
        compiler_params=pltpu.CompilerParams(vmem_limit_bytes=VMEM_LIMIT),
        cost_estimate=pl.CostEstimate(
            flops=8 * seg * seg * width, bytes_accessed=16 * seg * width, transcendentals=seg * seg * heads
        ),
        name="attend_new",
    )(queries, new_kv)


def attend_kernel(
    first_row, rows, last, steps, order_ref, length_ref, slot_ref, qt_ref, kv_ref, top_in, sum_in, acc_in, *refs
):
    bf16 = jnp.bfloat16
    outs, state = (refs[:1], refs[1:]) if last else ((), refs)
    single = last and steps == 1
    olds = (top_in, sum_in, acc_in) if single else None
    top_ref, sum_ref, acc_ref = state
    heads, _, seg = qt_ref.shape
    step = pl.program_id(0)
    sources = kv_ref.shape[0]
    block = sources * rows

    if not single:

        @pl.when(step == 0)
        def _():
            top_ref[...] = top_in[...]
            sum_ref[...] = sum_in[...]
            acc_ref[...] = acc_in[...]

    length = length_ref[order_ref[slot_ref[0]]]
    start = step * sources * ROWS + first_row
    end = start + (sources - 1) * ROWS + rows

    def block_of(which):
        return kv_ref[:, which].reshape(block, ATT_DIM)

    @pl.when(end <= length)
    def _():
        update(qt_ref, *state, block_of(0), block_of(1), None, False, olds)

    @pl.when((start < length) & (end > length))
    def _():
        row = lax.broadcasted_iota(jnp.int32, (block, seg), 0)
        place = start + row // rows * ROWS + row % rows
        update(qt_ref, *state, block_of(0), block_of(1), place < length, False, olds)

    if last:

        @pl.when(step == pl.num_programs(0) - 1)
        def _():
            for h in range(heads):
                result = acc_ref[h] / sum_ref[h : h + 1, :]
                outs[0][:, h * ATT_DIM : (h + 1) * ATT_DIM] = result.T.astype(bf16)


def attend(order, prefix_len, slot, qt, kv, carry, first_row, per, last):
    heads, _, seg = qt.shape
    sources, _, rows, _ = kv.shape

    def whole(shape):
        return pl.BlockSpec(shape, lambda i, *_: (0,) * len(shape))

    qt, *carry = [pltpu.with_memory_space_constraint(a, pltpu.HBM) for a in (qt, *carry)]
    carried = [a.shape for a in carry]
    outs = [(seg, heads * ATT_DIM)] if last else carried
    kind = jnp.bfloat16 if last else jnp.float32

    def at(i, order, lengths, slot):
        length = lengths[order[slot[0]]]
        return (jnp.minimum(i, (length - 1 - first_row) // (per * ROWS)), 0, 0, 0)

    work = sources * rows * seg * heads
    result = pl.pallas_call(
        functools.partial(attend_kernel, first_row, rows, last, sources // per),
        grid_spec=pltpu.PrefetchScalarGridSpec(
            num_scalar_prefetch=3,
            grid=(sources // per,),
            in_specs=[whole(qt.shape), pl.BlockSpec((per, 2, rows, ATT_DIM), at)]
            + [whole(s) for s in carried],
            out_specs=[whole(s) for s in outs],
            scratch_shapes=[pltpu.VMEM(s, jnp.float32) for s in carried] if last else [],
        ),
        out_shape=[pltpu.HBM(s, kind) for s in outs],
        compiler_params=pltpu.CompilerParams(vmem_limit_bytes=(32 if last else 56) * 1024 * 1024),
        cost_estimate=pl.CostEstimate(
            flops=64 * work * ATT_DIM, bytes_accessed=4 * sources * rows * ATT_DIM, transcendentals=work
        ),
        name="attend_chunk",
    )(order, prefix_len, slot, qt, kv, *carry)
    return result[0] if last else tuple(result)


def local(
    ssm_in,
    gate_in,
    b_in,
    c_in,
    dt_in,
    dt_bias,
    decay_rate,
    skip,
    norm_gain,
    out_weight,
    state_roll,
    query,
    new_kv,
    prefix_kv,
    prefix_len,
    order,
):
    slot = lax.axis_index("traj")
    own_state = lax.all_to_all(
        state_roll.at[order]
        .get(mode="promise_in_bounds", wrap_negative_indices=False)
        .astype(jnp.bfloat16),
        "traj", split_axis=0, concat_axis=0, tiled=True
    )
    prefix_kv = pltpu.with_memory_space_constraint(prefix_kv, pltpu.HBM)
    received, ahead = [], own_state
    for part in pack(order, prefix_kv):
        ahead, part = lax.optimization_barrier((ahead, part))
        if received:
            received[-1] = ahead
        else:
            own_state = ahead
        ahead = lax.all_to_all(part, ("traj", "tensor"), split_axis=0, concat_axis=0, tiled=True)
        received.append(ahead)
    heads = dt_in.shape[2]
    state = jnp.transpose(own_state, (1, 0, 2, 3)).reshape(heads * HEAD_DIM, STATE)
    place = lax.axis_index("tensor")
    core = place % 2
    tensor = lax.axis_size("tensor")
    other, normed, final_state = mixer(
        (1 - core)[None],
        ssm_in[0],
        gate_in[0],
        b_in[0],
        c_in[0],
        dt_in[0],
        dt_bias,
        decay_rate,
        skip,
        norm_gain,
        state,
        out_weight,
    )
    arrived = lax.ppermute(other, "tensor", [(i, i ^ 1) for i in range(tensor)])
    *carry, qt = attend_new(query[0], new_kv[:, 0])
    normed, carry[0] = lax.optimization_barrier((normed, carry[0]))
    mixed = lax.psum_scatter(
        project(core[None], normed, out_weight, arrived),
        "tensor",
        scatter_dimension=0,
        tiled=True,
        axis_index_groups=[list(range(c, tensor, 2)) for c in range(2)],
    )
    for number, (part, (first_row, _, per)) in enumerate(zip(received, CHUNKS)):
        last = number == len(CHUNKS) - 1
        carry = attend(order, prefix_len, slot[None], qt, part, carry, first_row, per, last)
    return (mixed, final_state.reshape(1, heads, HEAD_DIM, STATE), carry[None])


def solution(mesh):
    in_specs = (
        P("traj", None, "tensor"),
        P("traj", None, "tensor"),
        P("traj", None, "tensor"),
        P("traj", None, "tensor"),
        P("traj", None, "tensor"),
        P("tensor"),
        P("tensor"),
        P("tensor"),
        P("tensor"),
        P("tensor", None),
        P(None, "tensor", "traj", None),
        P("traj", None, "tensor"),
        P(None, "traj", None, "tensor"),
        P(None, None, ("traj", "tensor"), None),
        P(),
        P(),
    )
    out_specs = (
        P("traj", None, "tensor"),
        P("traj", "tensor", None, None),
        P("traj", None, "tensor"),
    )
    return jax.shard_map(local, mesh=mesh, in_specs=in_specs, out_specs=out_specs, check_vma=False)
```
